32 devices in a mesh: rank: 4 (over y, x), slab: 8 (over z, core).
Axes of the slice: x: 2, y: 2, z: 4, core: 2. Of those that a mesh axis runs over, the one named last changes fastest.
Arguments:
- chol_vectors: float32 [64, 1024, 1024], P('rank', 'slab'), may hold values from -6 to 6
- collocation: float32 [1024, 4096], P(None, 'slab'), may hold values from -0.1875 to 0.1875
- occupancy: int32 [8, 8], replicated, may hold values 0 or 1
Outputs:
- projected: float32 [64, 4096], P('rank', 'slab')
- gram: float32 [4096, 4096], P('slab', 'rank')
The draws below stay inside these ranges and needn't reach their ends.
All inputs are finite; a program needn't handle non-finite values.
Results may differ from the reference program's by a relative error of at most 0.00017.
Values sent between devices are 32-bit elements; how exact they have to be, the bound alone decides.
No kernel may reach another device: no remote copies, remote signals or barrier semaphores. Data moves between devices by JAX's collectives and lax.ppermute only.
A program may use at most 128 MiB of HBM per device.

```python
import jax
import jax.numpy as jnp
from jax import lax

NORB = 1024
TILE = 128
CHOL_DEV = 16
NTILE = 8
RANK = 4096
CHOLS = 64
N_RANK = 4


def plant(array, rng, smallest, largest):
    spot = [jax.random.randint(jax.random.fold_in(rng, axis), (), 0, length) for axis, length in enumerate(array.shape)]
    longest = array.shape.index(max(array.shape))
    neighbour = spot[:longest] + [(spot[longest] + 1) % array.shape[longest]] + spot[longest + 1:]
    return array.at[tuple(spot)].set(smallest).at[tuple(neighbour)].set(largest)


def block_levels(rng, dims, pieces, smallest, high):
    gain = 1.0
    for position, shards_of in pieces:
        steps = jax.random.uniform(jax.random.fold_in(jax.random.fold_in(rng, 6), position), (shards_of,), jnp.float32, smallest / len(pieces), high / len(pieces))
        gain = gain * jnp.repeat(jnp.exp(steps), dims[position] // shards_of).reshape((-1,) + (1,) * (len(dims) - 1 - position))
    return gain


def gaussian(rng, dims, spread, most, shards=(), held_as=jnp.bfloat16):
    array = jax.random.normal(rng, dims, jnp.float32) * spread
    if len(shards) > 0:
        array = block_levels(rng, dims, shards, -0.22, 0.18) * array
    return jnp.clip(array, min=-most, max=most).astype(held_as)


def setup_inputs(seed: int = 0) -> dict:
    streams_of = jax.random.split(jax.random.key(seed), 4)
    chol_vectors = gaussian(streams_of[0], (CHOLS, NORB, NORB), 1.0, 6.0, ((0, 4), (1, 8)), jnp.float32)
    collocation = gaussian(streams_of[1], (NORB, RANK), NORB ** -0.5, 0.1875, ((1, 8),), jnp.float32)
    occupancy = plant((jax.random.randint(streams_of[2], (NTILE, NTILE), 0, 4) < 3).astype(jnp.int32), jax.random.fold_in(streams_of[2], 1), 0, 1)
    return {"chol_vectors": chol_vectors, "collocation": collocation, "occupancy": occupancy}


def reference(chol_vectors, collocation, occupancy):
    mask_full = jnp.repeat(jnp.repeat(occupancy, TILE, axis=0), TILE, axis=1).astype(jnp.float32)

    def project_one(matrix):
        images = jnp.dot(matrix * mask_full, collocation, precision=lax.Precision.HIGHEST, preferred_element_type=jnp.float32)
        return jnp.sum(images * collocation, axis=0)

    projected = lax.map(project_one, chol_vectors)
    gram = jnp.dot(projected.T, projected, precision=lax.Precision.HIGHEST, preferred_element_type=jnp.float32)
    gram = gram / jnp.float32(CHOL_DEV * N_RANK)
    return projected, gram
```

```python
import functools

import jax
import jax.numpy as jnp
from jax import lax
from jax.experimental import pallas as pl
from jax.experimental.pallas import tpu as pltpu
from jax.sharding import PartitionSpec as P

TILE = 128
CORES = 2
AXES = ("rank", "slab")
VMEM_BYTES = 56 * 2**20


def split(values):
    high = values.astype(jnp.bfloat16)
    low = (values - high.astype(jnp.float32)).astype(jnp.bfloat16)
    return high, low


def product(high, low, point_high, point_low):
    return jnp.dot(
        jnp.concatenate([high, low, high], axis=1),
        jnp.concatenate([point_high, point_high, point_low], axis=0),
        preferred_element_type=jnp.float32,
    )


def first_kernel(flip, step, rows, occ_ref, a_ref, c_ref, high_ref, low_ref, out_ref, c_high, c_low):
    i = pl.program_id(0)
    slab = lax.axis_index("slab")
    slab = slab + flip * (1 - 2 * lax.rem(slab, CORES))

    @pl.when(i == 0)
    def _():
        c_high[...], c_low[...] = split(c_ref[...])

    grain = min(rows, TILE)
    for g in range(rows // grain):
        tile_row = (slab * rows + g * grain) // TILE
        for t in range(a_ref.shape[2] // TILE):
            part = (slice(None), slice(g * grain, (g + 1) * grain), slice(t * TILE, (t + 1) * TILE))
            masked = a_ref[part] * occ_ref[tile_row, t].astype(jnp.float32)
            high_ref[part], low_ref[part] = split(masked)
    flat = (step * rows, a_ref.shape[2])
    images = product(high_ref[...].reshape(flat), low_ref[...].reshape(flat), c_high[...], c_low[...])
    own = c_ref[pl.ds(pl.multiple_of(slab * rows, rows), rows), :]
    sums = jnp.sum(images.reshape(step, rows, -1) * own[None], axis=1)
    for p in range(step):
        out_ref[pl.ds(i * step + p, 1), :] = sums[p : p + 1]


def first_block(flip, a, c, occupancy):
    chols, rows, orbitals = a.shape
    step = 4
    points = c.shape[1]
    block = pl.BlockSpec((step, rows, orbitals), lambda i: (i, 0, 0))
    return pl.pallas_call(
        functools.partial(first_kernel, flip, step, rows),
        grid=(chols // step,),
        in_specs=[
            pl.BlockSpec(memory_space=pltpu.SMEM),
            block,
            pl.BlockSpec((orbitals, points), lambda i: (0, 0)),
        ],
        out_specs=[block, block, pl.BlockSpec((chols, points), lambda i: (0, 0))],
        out_shape=[
            jax.ShapeDtypeStruct(a.shape, jnp.bfloat16),
            jax.ShapeDtypeStruct(a.shape, jnp.bfloat16),
            jax.ShapeDtypeStruct((chols, points), jnp.float32),
        ],
        scratch_shapes=[pltpu.VMEM((orbitals, points), jnp.bfloat16)] * 2,
        compiler_params=pltpu.CompilerParams(vmem_limit_bytes=VMEM_BYTES),
        cost_estimate=pl.CostEstimate(
            flops=6 * chols * rows * orbitals * points, bytes_accessed=8 * a.size, transcendentals=0
        ),
    )(occupancy, a, c)


def next_kernel(places, step, rows, *refs):
    own_high, own_low, other_high, other_low = refs[:4]
    pieces = refs[4 : 4 + len(places)]
    out_ref, c_high, c_low, c_own, c_other = refs[4 + len(places) :]
    i = pl.program_id(0)
    rank, slab = lax.axis_index("rank"), lax.axis_index("slab")
    other = slab + 1 - 2 * lax.rem(slab, CORES)

    @pl.when(i == 0)
    def _():
        for (k, share, offset), piece in zip(places, pieces):
            count = piece.shape[0]
            at = pl.ds(pl.multiple_of((rank ^ k) * share + offset, count), count)
            c_high[at, :], c_low[at, :] = split(piece[...])
        for start, kept in ((slab, c_own), (other, c_other)):
            at = pl.ds(pl.multiple_of(start * rows, rows), rows)
            kept[...] = c_high[at, :].astype(jnp.float32) + c_low[at, :].astype(jnp.float32)

    flat = (step * rows, own_high.shape[2])
    total = None
    for high_ref, low_ref, kept in ((own_high, own_low, c_own), (other_high, other_low, c_other)):
        images = product(high_ref[...].reshape(flat), low_ref[...].reshape(flat), c_high[...], c_low[...])
        sums = jnp.sum(images.reshape(step, rows, -1) * kept[...][None], axis=1)
        total = sums if total is None else total + sums
    for p in range(step):
        out_ref[pl.ds(i * step + p, 1), :] = total[p : p + 1]


def next_block(own, other, places, pieces):
    chols, rows, orbitals = own[0].shape
    step = 2
    points = pieces[0].shape[1]
    block = pl.BlockSpec((step, rows, orbitals), lambda i: (i, 0, 0))
    return pl.pallas_call(
        functools.partial(next_kernel, places, step, rows),
        grid=(chols // step,),
        in_specs=[block] * 4 + [pl.BlockSpec(piece.shape, lambda i: (0, 0)) for piece in pieces],
        out_specs=pl.BlockSpec((chols, points), lambda i: (0, 0)),
        out_shape=jax.ShapeDtypeStruct((chols, points), jnp.float32),
        scratch_shapes=[pltpu.VMEM((orbitals, points), jnp.bfloat16)] * 2
        + [pltpu.VMEM((rows, points), jnp.float32)] * 2,
        compiler_params=pltpu.CompilerParams(vmem_limit_bytes=VMEM_BYTES),
        cost_estimate=pl.CostEstimate(
            flops=12 * chols * rows * orbitals * points, bytes_accessed=8 * own[0].size, transcendentals=0
        ),
    )(*own, *other, *pieces)


def combine_kernel(*refs):
    *pieces, out_ref = refs
    rank = lax.axis_index("rank")
    count = pieces[0].shape[0]
    for k, piece in enumerate(pieces):
        out_ref[pl.ds(pl.multiple_of((rank ^ k) * count, count), count), :] = piece[...]


def combine(pieces):
    chols, points = pieces[0].shape
    return pl.pallas_call(
        combine_kernel,
        out_shape=jax.ShapeDtypeStruct((len(pieces) * chols, points), jnp.float32),
    )(*pieces)


def gram_kernel(chols, rows_ref, same_ref, cross_ref, out_ref):
    core = lax.rem(lax.axis_index("slab"), CORES)
    points = same_ref.shape[1]
    rows_high, rows_low = split(rows_ref[...].T * jnp.float32(1.0 / chols))
    for place, ref in ((core, same_ref), (1 - core, cross_ref)):
        col_high, col_low = split(ref[...])
        out_ref[:, pl.ds(pl.multiple_of(place * points, points), points)] = product(
            rows_high, rows_low, col_high, col_low
        )


def gram_block(rows, same, cross):
    chols, points = rows.shape
    step = min(points, TILE)
    return pl.pallas_call(
        functools.partial(gram_kernel, chols),
        grid=(points // step,),
        in_specs=[
            pl.BlockSpec((chols, step), lambda i: (0, i)),
            pl.BlockSpec((chols, points), lambda i: (0, 0)),
            pl.BlockSpec((chols, points), lambda i: (0, 0)),
        ],
        out_specs=pl.BlockSpec((step, CORES * points), lambda i: (i, 0)),
        out_shape=jax.ShapeDtypeStruct((points, CORES * points), jnp.float32),
    )(rows, same, cross)


def per_device(chol_vectors, collocation, occupancy):
    ranks, slabs = lax.axis_size("rank"), lax.axis_size("slab")
    depth = slabs // CORES
    rank = lax.axis_index("rank")
    orbitals = collocation.shape[0]
    share = orbitals // ranks

    def move(value, place):
        pairs = []
        for r in range(ranks):
            for s in range(slabs):
                to_r, to_z, to_c = place(r, s // CORES, s % CORES)
                pairs.append((r * slabs + s, to_r * slabs + to_z * CORES + to_c))
        return lax.ppermute(value, AXES, pairs)

    def after(value, *others):
        return lax.optimization_barrier((value, *others))[0]

    def across(value, k):
        return move(value, lambda r, z, c: (r ^ k, z, c))

    def spread(piece):
        places, pieces = [(0, share, 0)], [piece]
        for k in range(1, ranks):
            places.append((k, share, 0))
            pieces.append(across(piece, k))
        return tuple(places), pieces

    order = list(range(1, depth, 2)) + list(range(2, depth, 2))
    piece = lax.dynamic_slice_in_dim(collocation, rank * share, share, 0)

    def fetch(k, token):
        source = piece if token is None else after(piece, token)
        return move(source, lambda r, z, c: (r, (z - k) % depth, c))

    arrived = fetch(order[0], None)
    other_chols = move(chol_vectors, lambda r, z, c: (r, z, 1 - c))
    *own, total = first_block(0, chol_vectors, collocation, occupancy)
    tokens = [total]
    *other, more = first_block(1, other_chols, collocation, occupancy)
    tokens.append(more)
    total = total + more
    for n, k in enumerate(order):
        places, pieces = spread(after(arrived, tokens[n]))
        if n + 1 < len(order):
            arrived = fetch(order[n + 1], tokens[n])
        partial = next_block(own, other, places, pieces)
        tokens.append(partial)
        total = total + move(partial, lambda r, z, c, k=k: (r, (z + k) % depth, c))
    projected = total

    rows = combine([projected] + [across(projected, k) for k in range(1, ranks)])
    same = move(rows, lambda r, z, c: (z, r, c))
    cross = move(rows, lambda r, z, c: (z, r ^ (ranks // 2), 1 - c))
    return projected, gram_block(rows, same, cross)


def solution(mesh):
    placed = (P("rank", "slab", None), P(None, "slab"), P())
    return jax.shard_map(
        per_device,
        mesh=mesh,
        in_specs=placed,
        out_specs=(P("rank", "slab"), P("slab", "rank")),
        check_vma=False,
    )
```

```python
import functools

import jax
import jax.numpy as jnp
from jax import lax
from jax.experimental import pallas as pl
from jax.experimental.pallas import tpu as pltpu
from jax.sharding import PartitionSpec as P

TILE = 128
CORES = 2
AXES = ("rank", "slab")
VMEM_BYTES = 20 * 2**20


def split(values):
    high = values.astype(jnp.bfloat16)
    return high, (values - high.astype(jnp.float32)).astype(jnp.bfloat16)


def product(left, right):
    left_high, left_low = left
    right_high, right_low = right
    return jnp.dot(
        jnp.concatenate([left_high, left_low, left_high], axis=1),
        jnp.concatenate([right_high, right_high, right_low], axis=0),
        preferred_element_type=jnp.float32,
    )


def row_sums(a_parts, c_refs, own):
    step, rows, orbitals = a_parts[0].shape
    images = product(
        [part.reshape(step * rows, orbitals) for part in a_parts], [ref[...] for ref in c_refs]
    )
    return jnp.sum(images.reshape(step, rows, -1) * own[None], axis=1)


def keep(value):
    return pltpu.with_memory_space_constraint(value, pltpu.HBM)


def first_kernel(flip, step, rows, occ_ref, a_ref, c_ref, *refs):
    a_refs, out_ref, c_refs = refs[:2], refs[2], refs[3:]
    i = pl.program_id(0)
    slab = lax.axis_index("slab")
    slab = slab + flip * (1 - 2 * lax.rem(slab, CORES))

    @pl.when(i == 0)
    def _():
        for ref, part in zip(c_refs, split(c_ref[...])):
            ref[...] = part

    grain = min(rows, TILE)
    now = pl.ds(i * step, step)
    for g in range(rows // grain):
        tile_row = (slab * rows + g * grain) // TILE
        for t in range(a_ref.shape[2] // TILE):
            at = (slice(None), slice(g * grain, (g + 1) * grain), slice(t * TILE, (t + 1) * TILE))
            masked = a_ref[at] * occ_ref[tile_row, t].astype(jnp.float32)
            for ref, part in zip(a_refs, split(masked)):
                ref[(now,) + at[1:]] = part
    own = c_ref[pl.ds(pl.multiple_of(slab * rows, rows), rows), :]
    sums = row_sums([ref[now] for ref in a_refs], c_refs, own)
    for p in range(step):
        out_ref[pl.ds(i * step + p, 1), :] = sums[p : p + 1]


def first_block(flip, a, c, occupancy, step=4):
    chols, rows, orbitals = a.shape
    points = c.shape[1]
    block = pl.BlockSpec((step, rows, orbitals), lambda i: (i, 0, 0))
    *a_parts, out = pl.pallas_call(
        functools.partial(first_kernel, flip, step, rows),
        grid=(chols // step,),
        in_specs=[
            pl.BlockSpec(memory_space=pltpu.SMEM),
            block,
            pl.BlockSpec((orbitals, points), lambda i: (0, 0)),
        ],
        out_specs=[pl.BlockSpec(memory_space=pltpu.VMEM)] * 2 + [pl.BlockSpec((chols, points), lambda i: (0, 0))],
        out_shape=[jax.ShapeDtypeStruct(a.shape, jnp.bfloat16)] * 2
        + [jax.ShapeDtypeStruct((chols, points), jnp.float32)],
        scratch_shapes=[pltpu.VMEM((orbitals, points), jnp.bfloat16)] * 2,
        compiler_params=pltpu.CompilerParams(vmem_limit_bytes=VMEM_BYTES),
        cost_estimate=pl.CostEstimate(
            flops=0, bytes_accessed=0, transcendentals=0
        ),
    )(keep(occupancy), keep(a), keep(c))
    return a_parts, out


def next_kernel(offsets, step, rows, *refs):
    own_refs, other_refs, pieces = refs[:2], refs[2:4], refs[4:-5]
    out_ref, *c_refs, c_own, c_other = refs[-5:]
    i = pl.program_id(0)
    rank, slab = lax.axis_index("rank"), lax.axis_index("slab")
    other = slab + 1 - 2 * lax.rem(slab, CORES)

    @pl.when(i == 0)
    def _():
        for offset, piece in zip(offsets, pieces):
            share = piece.shape[0]
            at = pl.ds(pl.multiple_of((rank ^ offset) * share, share), share)
            for ref, part in zip(c_refs, split(piece[...])):
                ref[at, :] = part
        for mine, kept in ((slab, c_own), (other, c_other)):
            at = pl.ds(pl.multiple_of(mine * rows, rows), rows)
            kept[...] = c_refs[0][at, :].astype(jnp.float32) + c_refs[1][at, :].astype(jnp.float32)

    now = pl.ds(i * step, step)
    total = row_sums([ref[now] for ref in own_refs], c_refs, c_own[...]) + row_sums(
        [ref[now] for ref in other_refs], c_refs, c_other[...]
    )
    for p in range(step):
        out_ref[pl.ds(i * step + p, 1), :] = total[p : p + 1]


def next_block(own, other, offsets, pieces, step=4):
    chols, rows, orbitals = own[0].shape
    points = pieces[0].shape[1]
    operands = (*own, *other, *pieces)
    return pl.pallas_call(
        functools.partial(next_kernel, offsets, step, rows),
        grid=(chols // step,),
        in_specs=[pl.BlockSpec(memory_space=pltpu.VMEM)] * len(operands),
        out_specs=pl.BlockSpec((chols, points), lambda i: (0, 0)),
        out_shape=jax.ShapeDtypeStruct((chols, points), jnp.float32),
        scratch_shapes=[pltpu.VMEM((orbitals, points), jnp.bfloat16)] * 2
        + [pltpu.VMEM((rows, points), jnp.float32)] * 2,
        compiler_params=pltpu.CompilerParams(vmem_limit_bytes=VMEM_BYTES),
        cost_estimate=pl.CostEstimate(
            flops=0, bytes_accessed=0, transcendentals=0
        ),
    )(*operands)


def combine_kernel(*refs):
    *pieces, out_ref = refs
    rank = lax.axis_index("rank")
    count = pieces[0].shape[0]
    for k, piece in enumerate(pieces):
        out_ref[pl.ds(pl.multiple_of((rank ^ k) * count, count), count), :] = piece[...]


def combine(pieces):
    chols, points = pieces[0].shape
    return pl.pallas_call(
        combine_kernel,
        out_shape=jax.ShapeDtypeStruct((len(pieces) * chols, points), jnp.float32),
        compiler_params=pltpu.CompilerParams(vmem_limit_bytes=VMEM_BYTES),
    )(*pieces)


def gram_kernel(chols, rows_ref, same_ref, cross_ref, out_ref):
    core = lax.rem(lax.axis_index("slab"), CORES)
    points = same_ref.shape[1]
    step = out_ref.shape[0]
    at = pl.ds(pl.multiple_of(pl.program_id(0) * step, step), step)
    row_parts = split(rows_ref[:, at].T * jnp.float32(1.0 / chols))
    for place, ref in ((core, same_ref), (1 - core, cross_ref)):
        out_ref[:, pl.ds(pl.multiple_of(place * points, points), points)] = product(row_parts, split(ref[...]))


def gram_block(rows, same, cross):
    chols, points = rows.shape
    step = points // 2
    return pl.pallas_call(
        functools.partial(gram_kernel, chols),
        grid=(points // step,),
        in_specs=[pl.BlockSpec(memory_space=pltpu.VMEM)] * 3,
        out_specs=pl.BlockSpec((step, CORES * points), lambda i: (i, 0)),
        out_shape=jax.ShapeDtypeStruct((points, CORES * points), jnp.float32),
        compiler_params=pltpu.CompilerParams(vmem_limit_bytes=VMEM_BYTES),
    )(rows, same, cross)


def per_device(chol_vectors, collocation, occupancy):
    ranks, slabs = lax.axis_size("rank"), lax.axis_size("slab")
    depth = slabs // CORES
    rank = lax.axis_index("rank")
    orbitals = collocation.shape[0]
    share = orbitals // ranks

    def move(value, place):
        pairs = []
        for r in range(ranks):
            for s in range(slabs):
                to_r, to_z, to_c = place(r, s // CORES, s % CORES)
                pairs.append((r * slabs + s, to_r * slabs + to_z * CORES + to_c))
        return lax.ppermute(value, AXES, pairs)

    def after(value, *others):
        return lax.optimization_barrier((value, *others))[0]

    def across(value, k):
        return move(value, lambda r, z, c: (r ^ k, z, c))

    def quarter(offset):
        return lax.dynamic_slice_in_dim(collocation, (rank ^ offset) * share, share, 0)

    def fetch(k, source):
        return move(source, lambda r, z, c: (r, (z - k) % depth, c))

    order = list(range(1, depth, 2)) + list(range(2, depth, 2))
    count = len(order)
    farthest = ranks - 1
    mine, far = quarter(0), quarter(farthest)
    held = {n: {} for n in range(count)}

    def begin(n, token):
        if n < count:
            held[n][0] = fetch(order[n], mine if token is None else after(mine, token))

    def exchange(n, *tokens):
        if n < count:
            source = after(held[n][0], *tokens)
            for k in range(1, ranks):
                if n == count - 1 and k == farthest:
                    held[n][k] = fetch(order[n], after(far, tokens[0]))
                else:
                    held[n][k] = across(source, k)

    begin(0, None)
    other_chols = move(chol_vectors, lambda r, z, c: (r, z, 1 - c))
    own, total = first_block(0, chol_vectors, collocation, occupancy)
    exchange(0, total)
    begin(1, total)
    other, more = first_block(1, other_chols, collocation, occupancy)
    exchange(1, more, *(held[0].values() if count else ()))
    begin(2, more)
    total = total + more
    for n, k in enumerate(order):
        partial = next_block(own, other, *zip(*((j, held[n][j]) for j in range(ranks))))
        exchange(n + 2, partial)
        begin(n + 3, partial)
        total = total + move(partial, lambda r, z, c, k=k: (r, (z + k) % depth, c))
    projected = total

    rows = combine([projected] + [across(projected, k) for k in range(1, ranks)])
    same = move(rows, lambda r, z, c: (z, r, c))
    cross = move(rows, lambda r, z, c: (z, r ^ (ranks // 2), 1 - c))
    return projected, gram_block(rows, same, cross)


def solution(mesh):
    placed = (P("rank", "slab", None), P(None, "slab"), P())
    return jax.shard_map(
        per_device,
        mesh=mesh,
        in_specs=placed,
        out_specs=(P("rank", "slab"), P("slab", "rank")),
        check_vma=False,
    )
```
